256 devices in a mesh: member: 16 (over y, x), region: 16 (over z, core).
Axes of the slice: x: 4, y: 4, z: 8, core: 2. Of those that a mesh axis runs over, the one named last changes fastest.
Arguments:
- states: float32 [512, 262144], P('member', 'region'), may hold values from -6 to 6
- obs_ens: float32 [512, 16384], P('member', 'region'), may hold values from -6 to 6
- innovation: float32 [512, 16384], P('member', 'region'), may hold values from -3 to 3
- lists: int32 [2048, 24], P('region'), may hold values from 0 to 127, as said below
- counts: int32 [2048], P('region'), may hold values from 1 to 24, as said below
- taper: float32 [2048, 24], P('region'), may hold values from 0.2 to 1
Outputs:
- analysis: float32 [512, 262144], P('member', 'region')
The draws below stay inside these ranges and needn't reach their ends.
Inputs may be any that keep to these rules, and one draw needn't show every extreme that they name: `lists`: cell block c lies in region r = c // (8 * 16); its listed ids name observation blocks of regions r - 1, r or r + 1 (those that exist), region q owning blocks q*8 to (q+1)*8 - 1; ids may repeat, and a repeat counts again. Entries at positions counts[c] and beyond of lists and taper are not used; some cell block uses all 24.
All inputs are finite; a program needn't handle non-finite values.
Results may differ from the reference program's by a relative error of at most 0.0003.
Values sent between devices are 32-bit elements; how exact they have to be, the bound alone decides.
A program may use at most 128 MiB of HBM per device.

```python
import jax
import jax.numpy as jnp
from jax import lax

M = 512
BLK = 128
L = 24
OBR = 8
NCB = 2048
NC = 262144
NOB = 128
NOBS = 16384


def draw_lists(key, part):
    key = jax.random.fold_in(key, 11)
    regions = NOB // OBR
    per_region = NCB // regions
    region_of = jnp.arange(NCB, dtype=jnp.int32) // per_region
    lower = jnp.maximum(region_of - 1, 0) * OBR
    upper = jnp.minimum(region_of + 2, regions) * OBR
    raw = jax.random.randint(key, (NCB, L), 0, 1 << 20, dtype=jnp.int32)
    return lower[:, None] + raw % (upper - lower)[:, None]


def draw_counts(key, part):
    key = jax.random.fold_in(key, 23)
    first, second, third = jax.random.split(key, 3)
    regions = NOB // OBR
    per_region = NCB // regions
    index = jnp.arange(NCB, dtype=jnp.int32)
    region_of = index // per_region
    offset = index % per_region
    starts = jax.random.randint(first, (regions,), 0, per_region, dtype=jnp.int32)
    run_length = max(per_region // 4, 1)
    heavy = (offset - starts[region_of]) % per_region < run_length
    light_count = jax.random.randint(second, (NCB,), 1, L // 3 + 1, dtype=jnp.int32)
    heavy_count = jax.random.randint(third, (NCB,), L * 3 // 4, L + 1, dtype=jnp.int32)
    result = jnp.where(heavy, heavy_count, light_count)
    return jnp.where(index == starts[0], L, result).astype(jnp.int32)


def steps_of(own_key, extent, cuts, least, high):
    level = 1.0
    for dim, shards_of in cuts:
        draws = jax.random.uniform(jax.random.fold_in(jax.random.fold_in(own_key, 6), dim), (shards_of,), jnp.float32, least / len(cuts), high / len(cuts))
        level = level * jnp.repeat(jnp.exp(draws), extent[dim] // shards_of).reshape((-1,) + (1,) * (len(extent) - 1 - dim))
    return level


def noise(own_key, dims, scale, most, pieces=(), kind=jnp.bfloat16):
    factor_of = steps_of(own_key, dims, pieces, -0.22, 0.18) if pieces else 1.0
    array = jax.random.normal(own_key, dims, jnp.float32) * scale * factor_of
    return jnp.minimum(jnp.maximum(array, -most), most).astype(kind)


def setup_inputs(seed: int = 0) -> dict:
    key_of = jax.random.split(jax.random.key(seed), 7)
    return {
        "states": noise(key_of[0], (M, NC), 1.0, 6.0, ((0, 16), (1, 16)), jnp.float32),
        "obs_ens": noise(key_of[1], (M, NOBS), 1.0, 6.0, ((0, 16), (1, 16)), jnp.float32),
        "innovation": noise(key_of[2], (M, NOBS), 0.5, 3.0, ((0, 16), (1, 16)), jnp.float32),
        "lists": draw_lists(jax.random.fold_in(key_of[6], 71), 0),
        "counts": draw_counts(jax.random.fold_in(key_of[6], 71), 0),
        "taper": jnp.clip(0.2 + 0.8 * jax.random.uniform(key_of[5], (NCB, L), jnp.float32) ** steps_of(key_of[5], (NCB, L), ((0, 16),), -0.2, 0.2), 0.2, 1.0),
    }


def reference(states, obs_ens, innovation, lists, counts, taper):
    anomalies = states - jnp.mean(states, axis=0, keepdims=True)
    obs_anom = obs_ens - jnp.mean(obs_ens, axis=0, keepdims=True)
    obs_blocks = obs_anom.reshape(M, NOB, BLK)
    inn_blocks = innovation.reshape(M, NOB, BLK)
    highest = lax.Precision.HIGHEST

    def one_block(position):
        column = lax.dynamic_slice_in_dim(anomalies, (position * BLK).astype(jnp.int32), BLK, 1)
        block_ids = lists[position]
        picked_obs = obs_blocks[:, block_ids, :]
        picked_inn = inn_blocks[:, block_ids, :]
        in_use = jnp.arange(L, dtype=jnp.int32) < counts[position]
        weights = jnp.where(in_use, taper[position], jnp.float32(0.0))
        cross = jnp.einsum("mjo,mc->joc", picked_obs, column, precision=highest)
        cross = cross * weights[:, None, None]
        return jnp.einsum("mjo,joc->mc", picked_inn, cross, precision=highest) / (M - 1.0)

    increments = lax.map(one_block, jnp.arange(NCB, dtype=jnp.int32))
    increment = jnp.transpose(increments, (1, 0, 2)).reshape(M, NC)
    return states + increment
```

```python
import jax
import jax.numpy as jnp
from jax import lax
from jax.experimental import pallas as pl
from jax.experimental.pallas import tpu as pltpu
from jax.sharding import PartitionSpec as P

MESH = pl.DeviceIdType.MESH
BLK = 128
NX = 4
NY = 4
GROUP = NX * NY
ROWS = 32
MEMBERS = 512
CELLS = 1024
CB = CELLS // BLK
OBS = 1024
OB = OBS // BLK
HALF = OBS // 2
L = 24
SENDS = 4
WIDE = CELLS // SENDS


def split(value):
    high = value.astype(jnp.bfloat16)
    return high, (value - high.astype(jnp.float32)).astype(jnp.bfloat16)


def kernel(
    states, obs, inn, lists, counts, taper, out,
    wide, cols, cells_hl, g, w, table, result,
    local_sem, g_send, g_recv, f_send, f_recv, a_send, a_recv, o_send, o_recv,
):
    member = lax.axis_index("member")
    region = lax.axis_index("region")
    regions = lax.axis_size("region")
    y, x = member // NX, member % NX
    core = region % 2
    above = lax.rem(region + 1, regions)
    below = lax.rem(region + regions - 1, regions)

    def at(yy, xx):
        return (lax.rem(yy, NY) * NX + lax.rem(xx, NX), region)

    own_obs = pltpu.make_async_copy(obs, wide.at[1, 0, y, x], local_sem.at[0])
    own_inn = pltpu.make_async_copy(inn, wide.at[1, 1, y, x], local_sem.at[1])
    own_cols = pltpu.make_async_copy(
        states.at[:, pl.ds(pl.multiple_of(member * CELLS, CELLS), CELLS)], cols.at[member], local_sem.at[2]
    )
    own_obs.start()
    own_inn.start()
    own_cols.start()

    barrier = pltpu.get_barrier_semaphore()
    for k in range(1, GROUP):
        pl.semaphore_signal(barrier, inc=1, device_id=at(y + k // NX, x + k % NX), device_id_type=MESH)
    for other in (above, below):
        pl.semaphore_signal(barrier, inc=1, device_id=(member, other), device_id_type=MESH)
    pl.semaphore_wait(barrier, GROUP + 1)

    first_half, second_half = pl.ds(0, HALF), pl.ds(HALF, HALF)

    def remote(source, target, send, recv, device):
        return pltpu.make_async_remote_copy(
            src_ref=source, dst_ref=target, send_sem=send, recv_sem=recv, device_id=device, device_id_type=MESH
        )

    def gather(phase, half, d):
        if phase == 0:
            piece = wide.at[1, :, y, x, :, first_half if half == 0 else second_half]
        elif half == 0:
            piece = wide.at[1, :, y, :, :, first_half]
        else:
            piece = wide.at[1, :, :, x, :, second_half]
        along_x = (phase == 0) == (half == 0)
        n = phase * 6 + half * 3 + d - 1
        return remote(piece, piece, g_send.at[n], g_recv.at[n], at(y, x + d) if along_x else at(y + d, x))

    def piece_of(slot, piece):
        if piece == 0:
            return wide.at[slot, :, y, x]
        phase, half, d = (piece - 1) // 6, (piece - 1) // 3 % 2, (piece - 1) % 3 + 1
        cut = first_half if half == 0 else second_half
        yy, xx = lax.rem(y + NY - d, NY), lax.rem(x + NX - d, NX)
        if phase == 0:
            return wide.at[slot, :, y, xx, :, cut] if half == 0 else wide.at[slot, :, yy, x, :, cut]
        return wide.at[slot, :, yy, :, :, cut] if half == 0 else wide.at[slot, :, :, xx, :, cut]

    def pass_on(piece, slot, n):
        return remote(
            piece_of(1, piece), piece_of(slot, piece), f_send.at[n, piece], f_recv.at[n, piece],
            (member, above if n == 0 else below),
        )

    def cells_in(k):
        yy, xx = lax.rem(y + k // NX, NY), lax.rem(x + k % NX, NX)
        target = yy * NX + xx
        return remote(
            states.at[:, pl.ds(pl.multiple_of(target * CELLS, CELLS), CELLS)], cols.at[member],
            a_send.at[k - 1], a_recv.at[k - 1], (target, region),
        )

    def cells_out(part, k):
        yy, xx = lax.rem(y + k // NX, NY), lax.rem(x + k % NX, NX)
        target = yy * NX + xx
        place = pl.multiple_of(member * CELLS + part * WIDE, WIDE)
        return remote(
            result.at[target, :, pl.ds(part * WIDE, WIDE)], out.at[:, pl.ds(place, WIDE)],
            o_send.at[part, k - 1], o_recv.at[part, k - 1], (target, region),
        )

    def both(piece):
        pass_on(piece, 0, 0).start()
        pass_on(piece, 2, 1).start()

    own_obs.wait()
    own_inn.wait()
    for d in (1, 3, 2):
        for half in (0, 1):
            gather(0, half, d).start()
    both(0)
    for d in (1, 3, 2):
        for half in (0, 1):
            gather(0, half, d).wait_recv()
            both(1 + half * 3 + d - 1)
    for d in (1, 3, 2):
        for half in (0, 1):
            gather(1, half, d).start()
    for k in range(1, GROUP):
        cells_in(k).start()

    start = pl.multiple_of(member * CB, CB)
    ids = lists[pl.ds(start, CB), :] - (region - 1) * OB
    rows = lax.broadcasted_iota(jnp.int32, (CB, L), 0)
    used = jnp.zeros((CB, L), jnp.int32)
    for i in range(CB):
        used = jnp.where(rows == i, counts[start + i], used)
    in_use = lax.broadcasted_iota(jnp.int32, (CB, L), 1) < used
    weights = jnp.where(in_use, taper[pl.ds(start, CB), :], 0.0) * (1.0 / (MEMBERS - 1.0))
    for b in range(3 * OB):
        total = jnp.sum(jnp.where(ids == b, weights, 0.0), axis=1, keepdims=True)
        table[b] = jnp.broadcast_to(total, (CB, BLK))

    for d in (1, 3, 2):
        for half in (0, 1):
            gather(1, half, d).wait_recv()
            both(7 + half * 3 + d - 1)

    def window(slot, first):
        def block(b, carry):
            at_b = pl.ds(pl.multiple_of(b * BLK, BLK), BLK)
            o = wide[slot, 0, :, :, :, at_b].reshape(MEMBERS, BLK)
            o_hi, o_lo = split(o - jnp.mean(o, axis=0, keepdims=True))
            i_hi, i_lo = split(wide[slot, 1, :, :, :, at_b].reshape(MEMBERS, BLK))
            g[b] = lax.dot_general(
                jnp.concatenate([i_hi, i_lo, i_hi], axis=1), jnp.concatenate([o_hi, o_hi, o_lo], axis=1),
                (((1,), (1,)), ((), ())), preferred_element_type=jnp.float32,
            )
            return carry

        lax.fori_loop(0, OB, block, 0)

        def strip(i, carry):
            at_i = pl.ds(pl.multiple_of(i * 8, 8), 8)
            lanes = [pl.ds(k * BLK, BLK) for k in range(MEMBERS // BLK)]
            parts = [[g[b, at_i, lane] for lane in lanes] for b in range(OB)]
            for c in range(CB):
                sums = [None if first else w[c, at_i, lane] for lane in lanes]
                for b in range(OB):
                    weight = jnp.broadcast_to(table[slot * OB + b, pl.ds(c, 1), :], (8, BLK))
                    sums = [
                        part * weight if old is None else old + part * weight for old, part in zip(sums, parts[b])
                    ]
                for lane, new in zip(lanes, sums):
                    w[c, at_i, lane] = new
            return carry

        lax.fori_loop(0, MEMBERS // 8, strip, 0)

    window(1, True)
    near, far = 2 - 2 * core, 2 * core
    for piece in range(13):
        pass_on(piece, 0, 0).wait_send()
        pass_on(piece, 2, 1).wait_send()

    def arrived(slot):
        for piece in range(13):
            target = piece_of(slot, piece)
            remote(
                target, target, f_send.at[slot // 2, piece], f_recv.at[slot // 2, piece], (member, above)
            ).wait_recv()

    arrived(near)
    window(near, False)

    own_cols.wait()
    for k in range(1, GROUP):
        cells_in(k).wait_recv()

    def centre(c, carry):
        at_c = pl.ds(pl.multiple_of(c * BLK, BLK), BLK)
        a = cols[:, :, at_c].reshape(MEMBERS, BLK)
        hi, lo = split(a - jnp.mean(a, axis=0, keepdims=True))
        cells_hl[c] = jnp.concatenate([hi, lo], axis=1)
        return carry

    lax.fori_loop(0, CB, centre, 0)

    arrived(far)
    window(far, False)

    own_out = []
    for part in range(SENDS):
        def finish(c, carry):
            at_c = pl.ds(pl.multiple_of(c * BLK, BLK), BLK)
            hi, lo = split(w[c])
            a = cells_hl[c]
            both_ = jnp.dot(hi, a, preferred_element_type=jnp.float32)
            low = jnp.dot(lo, a[:, :BLK], preferred_element_type=jnp.float32)
            inc = both_[:, :BLK] + (both_[:, BLK:] + low)
            result[:, :, at_c] = cols[:, :, at_c] + inc.reshape(GROUP, ROWS, BLK)
            return carry

        lax.fori_loop(part * (CB // SENDS), (part + 1) * (CB // SENDS), finish, 0)
        for k in range(1, GROUP):
            cells_out(part, k).start()
    place = pl.multiple_of(member * CELLS, CELLS)
    keep = pltpu.make_async_copy(result.at[member], out.at[:, pl.ds(place, CELLS)], local_sem.at[3])
    keep.start()

    for phase in (0, 1):
        for half in (0, 1):
            for d in (1, 2, 3):
                gather(phase, half, d).wait_send()
    for k in range(1, GROUP):
        cells_in(k).wait_send()
    for part in range(SENDS):
        for k in range(1, GROUP):
            cells_out(part, k).wait()
    keep.wait()


def local(states, obs_ens, innovation, lists, counts, taper):
    hbm = pl.BlockSpec(memory_space=pl.ANY)
    vmem = pl.BlockSpec(memory_space=pltpu.VMEM)
    smem = pl.BlockSpec(memory_space=pltpu.SMEM)
    dma = pltpu.SemaphoreType.DMA
    return pl.pallas_call(
        kernel,
        out_shape=jax.ShapeDtypeStruct(states.shape, jnp.float32),
        in_specs=[hbm, hbm, hbm, vmem, smem, vmem],
        out_specs=hbm,
        scratch_shapes=[
            pltpu.VMEM((3, 2, NY, NX, ROWS, OBS), jnp.float32),
            pltpu.VMEM((GROUP, ROWS, CELLS), jnp.float32),
            pltpu.VMEM((CB, MEMBERS, 2 * BLK), jnp.bfloat16),
            pltpu.VMEM((OB, MEMBERS, MEMBERS), jnp.float32),
            pltpu.VMEM((CB, MEMBERS, MEMBERS), jnp.float32),
            pltpu.VMEM((3 * OB, CB, BLK), jnp.float32),
            pltpu.VMEM((GROUP, ROWS, CELLS), jnp.float32),
            dma((4,)),
            dma((12,)),
            dma((12,)),
            dma((2, 13)),
            dma((2, 13)),
            dma((GROUP - 1,)),
            dma((GROUP - 1,)),
            dma((SENDS, GROUP - 1)),
            dma((SENDS, GROUP - 1)),
        ],
        compiler_params=pltpu.CompilerParams(
            collective_id=0, has_side_effects=True, vmem_limit_bytes=56 * 2**20
        ),
        name="analysis",
    )(states, obs_ens, innovation, lists, counts, taper)


def solution(mesh):
    return jax.shard_map(
        local,
        mesh=mesh,
        in_specs=(
            P("member", "region"),
            P("member", "region"),
            P("member", "region"),
            P("region", None),
            P("region"),
            P("region", None),
        ),
        out_specs=P("member", "region"),
        check_vma=False,
    )
```

```python
import jax
import jax.numpy as jnp
from jax import lax
from jax.experimental import pallas as pl
from jax.experimental.pallas import tpu as pltpu
from jax.sharding import PartitionSpec as P

MESH = pl.DeviceIdType.MESH
BLK = 128
NX = 4
NY = 4
GROUP = NX * NY
ROWS = 32
MEMBERS = 512
CELLS = 1024
CB = CELLS // BLK
OBS = 1024
OB = OBS // BLK
QUART = OBS // 4
QB = OB // 2
L = 24
SENDS = 4
ORDER = (1, 4, 3, 12, 5, 15, 7, 13, 2, 8, 6, 9, 14, 11, 10)
WIDE = CELLS // SENDS


def split(value):
    high = value.astype(jnp.bfloat16)
    return high, (value - high.astype(jnp.float32)).astype(jnp.bfloat16)


def kernel(
    states, obs, inn, lists, counts, taper, out,
    wide, cols, cells_hl, g, w, table, result,
    local_sem, g_send, g_recv, f_send, f_recv, a_send, a_recv, o_send, o_recv,
):
    member = lax.axis_index("member")
    region = lax.axis_index("region")
    regions = lax.axis_size("region")
    y, x = member // NX, member % NX
    core = region % 2
    above = lax.rem(region + 1, regions)
    below = lax.rem(region + regions - 1, regions)

    def at(yy, xx):
        return (lax.rem(yy, NY) * NX + lax.rem(xx, NX), region)

    own_obs = pltpu.make_async_copy(obs, wide.at[1, 0, y, x], local_sem.at[0])
    own_inn = pltpu.make_async_copy(inn, wide.at[1, 1, y, x], local_sem.at[1])
    own_cols = pltpu.make_async_copy(
        states.at[:, pl.ds(pl.multiple_of(member * CELLS, CELLS), CELLS)], cols.at[member], local_sem.at[2]
    )
    own_obs.start()
    own_inn.start()
    own_cols.start()

    barrier = pltpu.get_barrier_semaphore()
    for k in range(1, GROUP):
        pl.semaphore_signal(barrier, inc=1, device_id=at(y + k // NX, x + k % NX), device_id_type=MESH)
    for other in (above, below):
        pl.semaphore_signal(barrier, inc=1, device_id=(member, other), device_id_type=MESH)
    pl.semaphore_wait(barrier, GROUP + 1)

    def cut(q):
        return pl.ds(q * QUART, QUART)

    def remote(source, target, send, recv, device):
        return pltpu.make_async_remote_copy(
            src_ref=source, dst_ref=target, send_sem=send, recv_sem=recv, device_id=device, device_id_type=MESH
        )

    def line(slot, q, d):
        if q % 2 == 0:
            return wide.at[slot, :, y, lax.rem(x + d, NX), :, cut(q)]
        return wide.at[slot, :, lax.rem(y + d, NY), x, :, cut(q)]

    def plane(slot, q, d, kind=slice(None)):
        if q % 2 == 0:
            return wide.at[slot, kind, lax.rem(y + d, NY), :, :, cut(q)]
        return wide.at[slot, kind, :, lax.rem(x + d, NX), :, cut(q)]

    def along(q, hop, d):
        return at(y, x + d) if (q + hop) % 2 == 0 else at(y + d, x)

    def first(q, d):
        piece = line(1, q, 0)
        return remote(piece, piece, g_send.at[q, d - 1], g_recv.at[q, d - 1], along(q, 0, d))

    def second(q, d):
        piece = plane(1, q, 0)
        return remote(piece, piece, g_send.at[q, 2 + d], g_recv.at[q, 2 + d], along(q, 1, d))

    def relay(q, d):
        piece = plane(1, q, 4 - d, d // 2)
        return remote(piece, piece, g_send.at[q, 6 + d // 2], g_recv.at[q, 6 + d // 2], along(q, 1, d))

    def piece_of(slot, piece):
        if piece == 0:
            return wide.at[slot, :, y, x]
        if piece < 13:
            return line(slot, (piece - 1) // 3, (piece - 1) % 3 + 1)
        return plane(slot, (piece - 13) // 3, (piece - 13) % 3 + 1)

    def pass_on(piece, slot, n):
        return remote(
            piece_of(1, piece), piece_of(slot, piece), f_send.at[n, piece], f_recv.at[n, piece],
            (member, above if n == 0 else below),
        )

    def cells_in(k):
        yy, xx = lax.rem(y + k // NX, NY), lax.rem(x + k % NX, NX)
        target = yy * NX + xx
        return remote(
            states.at[:, pl.ds(pl.multiple_of(target * CELLS, CELLS), CELLS)], cols.at[member],
            a_send.at[k - 1], a_recv.at[k - 1], (target, region),
        )

    def cells_out(part, k):
        yy, xx = lax.rem(y + k // NX, NY), lax.rem(x + k % NX, NX)
        target = yy * NX + xx
        place = pl.multiple_of(member * CELLS + part * WIDE, WIDE)
        return remote(
            result.at[target, :, pl.ds(part * WIDE, WIDE)], out.at[:, pl.ds(place, WIDE)],
            o_send.at[part, k - 1], o_recv.at[part, k - 1], (target, region),
        )

    def both(piece):
        pass_on(piece, 0, 0).start()
        pass_on(piece, 2, 1).start()

    def lines(pair):
        for d in (1, 3, 2):
            for q in pair:
                first(q, d).wait_recv()
                both(3 * q + 4 - d)
        for d in (1, 3):
            for q in pair:
                second(q, d).start()

    def planes_near(pair, onward=None):
        for d in (1, 3):
            for q in pair:
                second(q, d).wait_recv()
                relay(q, d).start()
                if onward is None or q in onward:
                    both(13 + 3 * q + 3 - d)

    def planes_far(pair, last=()):
        for q in pair:
            for d in (1, 3):
                relay(q, d).wait_recv()
            both(13 + 3 * q + 1)
            if q in last[1:]:
                both(13 + 3 * q)
                both(13 + 3 * q + 2)

    own_obs.wait()
    own_inn.wait()
    for pair in ((0, 1), (2, 3)):
        for d in (1, 3, 2):
            for q in pair:
                first(q, d).start()
    both(0)
    lines((0, 1))
    lines((2, 3))

    start = member * CB
    ids = lists[...] - (region - 1) * OB
    used = lax.broadcasted_iota(jnp.int32, (L, BLK), 0) < counts[...]
    weights = jnp.where(used, taper[...], 0.0) * (1.0 / (MEMBERS - 1.0))
    lane_of = lax.broadcasted_iota(jnp.int32, (CB, BLK), 1)
    mine = (lane_of == start + lax.broadcasted_iota(jnp.int32, (CB, BLK), 0)).astype(jnp.float32)
    for b in range(3 * OB):
        total = jnp.sum(jnp.where(ids == b, weights, 0.0), axis=0, keepdims=True)
        table[b] = jnp.broadcast_to(jnp.sum(mine * total, axis=1, keepdims=True), (CB, BLK))

    def products(runs):
        base = 0
        for slot, begin, many in runs:
            def block(b, carry, slot=slot, begin=begin, base=base):
                at_b = pl.ds(pl.multiple_of((begin + b) * BLK, BLK), BLK)
                o = wide[slot, 0, :, :, :, at_b].reshape(MEMBERS, BLK)
                o_hi, o_lo = split(o - jnp.mean(o, axis=0, keepdims=True))
                i_hi, i_lo = split(wide[slot, 1, :, :, :, at_b].reshape(MEMBERS, BLK))
                g[base + b] = lax.dot_general(
                    jnp.concatenate([i_hi, i_lo, i_hi], axis=1), jnp.concatenate([o_hi, o_hi, o_lo], axis=1),
                    (((1,), (1,)), ((), ())), preferred_element_type=jnp.float32,
                )
                return carry

            lax.fori_loop(0, many, block, 0, unroll=True)
            base += many

    def add(runs, new=False):
        rows = [slot * OB + begin + b for slot, begin, many in runs for b in range(many)]

        def strip(i, carry):
            at_i = pl.ds(pl.multiple_of(i * 8, 8), 8)
            lanes = [pl.ds(k * BLK, BLK) for k in range(MEMBERS // BLK)]
            parts = [[g[b, at_i, lane] for lane in lanes] for b in range(len(rows))]
            for c in range(CB):
                sums = [None if new else w[c, at_i, lane] for lane in lanes]
                for row, part in zip(rows, parts):
                    weight = jnp.broadcast_to(table[row, pl.ds(c, 1), :], (8, BLK))
                    sums = [p * weight if old is None else old + p * weight for old, p in zip(sums, part)]
                for lane, total in zip(lanes, sums):
                    w[c, at_i, lane] = total
            return carry

        lax.fori_loop(0, MEMBERS // 8, strip, 0, unroll=2)

    def window(*runs):
        products(runs)
        add(runs)

    near, far = 2 - 2 * core, 2 * core

    def arrived(slot, pieces):
        for piece in pieces:
            target = piece_of(slot, piece)
            remote(
                target, target, f_send.at[slot // 2, piece], f_recv.at[slot // 2, piece], (member, above)
            ).wait_recv()

    early = (*range(7), *range(13, 19))
    planes_near((0, 1))
    planes_far((0, 1))
    products([(1, 0, 4)])
    planes_near((2, 3), (2,))
    add([(1, 0, 4)], True)
    planes_far((2, 3), (2, 3))
    for k in ORDER:
        cells_in(k).start()
    arrived(near, early)
    window((near, 0, 4))
    arrived(near, (*range(7, 13), *range(19, 25)))
    window((1, 4, 4), (near, 4, 4))
    arrived(far, early)
    window((far, 0, 4))

    own_cols.wait()
    for k in range(1, GROUP):
        cells_in(k).wait_recv()

    def centre(c, carry):
        at_c = pl.ds(pl.multiple_of(c * BLK, BLK), BLK)
        a = cols[:, :, at_c].reshape(MEMBERS, BLK)
        hi, lo = split(a - jnp.mean(a, axis=0, keepdims=True))
        cells_hl[c] = jnp.concatenate([hi, lo], axis=1)
        return carry

    lax.fori_loop(0, CB, centre, 0)

    arrived(far, (*range(7, 10), *range(19, 22)))
    window((far, 4, 2))
    arrived(far, (*range(10, 13), *range(22, 25)))
    window((far, 6, 2))

    for part in range(SENDS):
        def finish(c, carry):
            at_c = pl.ds(pl.multiple_of(c * BLK, BLK), BLK)
            hi, lo = split(w[c])
            a = cells_hl[c]
            both_ = jnp.dot(hi, a, preferred_element_type=jnp.float32)
            low = jnp.dot(lo, a[:, :BLK], preferred_element_type=jnp.float32)
            inc = both_[:, :BLK] + (both_[:, BLK:] + low)
            result[:, :, at_c] = cols[:, :, at_c] + inc.reshape(GROUP, ROWS, BLK)
            return carry

        lax.fori_loop(part * (CB // SENDS), (part + 1) * (CB // SENDS), finish, 0)
        for k in ORDER:
            cells_out(part, k).start()
    place = pl.multiple_of(member * CELLS, CELLS)
    keep = pltpu.make_async_copy(result.at[member], out.at[:, pl.ds(place, CELLS)], local_sem.at[3])
    keep.start()

    for q in range(4):
        for d in (1, 2, 3):
            first(q, d).wait_send()
        for d in (1, 3):
            second(q, d).wait_send()
            relay(q, d).wait_send()
    for piece in range(25):
        pass_on(piece, 0, 0).wait_send()
        pass_on(piece, 2, 1).wait_send()
    for k in range(1, GROUP):
        cells_in(k).wait_send()
    for part in range(SENDS):
        for k in range(1, GROUP):
            cells_out(part, k).wait()
    keep.wait()


def local(states, obs_ens, innovation, lists, counts, taper):
    hbm = pl.BlockSpec(memory_space=pl.ANY)
    vmem = pl.BlockSpec(memory_space=pltpu.VMEM)
    dma = pltpu.SemaphoreType.DMA
    return pl.pallas_call(
        kernel,
        out_shape=jax.ShapeDtypeStruct(states.shape, jnp.float32),
        in_specs=[hbm, hbm, hbm, vmem, vmem, vmem],
        out_specs=hbm,
        scratch_shapes=[
            pltpu.VMEM((3, 2, NY, NX, ROWS, OBS), jnp.float32),
            pltpu.VMEM((GROUP, ROWS, CELLS), jnp.float32),
            pltpu.VMEM((CB, MEMBERS, 2 * BLK), jnp.bfloat16),
            pltpu.VMEM((OB, MEMBERS, MEMBERS), jnp.float32),
            pltpu.VMEM((CB, MEMBERS, MEMBERS), jnp.float32),
            pltpu.VMEM((3 * OB, CB, BLK), jnp.float32),
            pltpu.VMEM((GROUP, ROWS, CELLS), jnp.float32),
            dma((4,)),
            dma((4, 8)),
            dma((4, 8)),
            dma((2, 25)),
            dma((2, 25)),
            dma((GROUP - 1,)),
            dma((GROUP - 1,)),
            dma((SENDS, GROUP - 1)),
            dma((SENDS, GROUP - 1)),
        ],
        compiler_params=pltpu.CompilerParams(
            collective_id=0, has_side_effects=True, vmem_limit_bytes=56 * 2**20
        ),
        name="analysis",
    )(states, obs_ens, innovation, lists.T, counts.reshape(1, -1), taper.T)


def solution(mesh):
    return jax.shard_map(
        local,
        mesh=mesh,
        in_specs=(
            P("member", "region"),
            P("member", "region"),
            P("member", "region"),
            P("region", None),
            P("region"),
            P("region", None),
        ),
        out_specs=P("member", "region"),
        check_vma=False,
    )
```

```python
import jax
import jax.numpy as jnp
from jax import lax
from jax.experimental import pallas as pl
from jax.experimental.pallas import tpu as pltpu
from jax.sharding import PartitionSpec as P

MESH = pl.DeviceIdType.MESH
BLK = 128
NX = 4
NY = 4
GROUP = NX * NY
ROWS = 32
MEMBERS = 512
CELLS = 1024
CB = CELLS // BLK
OBS = 1024
OB = OBS // BLK
QUART = OBS // 4
INS = 2
PART_IN = CELLS // INS
L = 24
PARTS = ((0, 2), (2, 2), (4, 2), (6, 2))
SENDS = len(PARTS)
EARLY = (0, 0, 0)
INS_EARLY = 1
ORDER = (1, 4, 3, 12, 5, 15, 7, 13, 2, 8, 6, 9, 14, 11, 10)


def split(value):
    high = value.astype(jnp.bfloat16)
    return high, (value - high.astype(jnp.float32)).astype(jnp.bfloat16)


def kernel(
    states, obs, inn, lists, counts, taper, out,
    wide, cols, cells_hl, g, w, table, result,
    local_sem, g_send, g_recv, f_send, f_recv, a_send, a_recv, o_send, o_recv,
):
    member = lax.axis_index("member")
    region = lax.axis_index("region")
    regions = lax.axis_size("region")
    y, x = member // NX, member % NX
    core = region % 2
    above = lax.rem(region + 1, regions)
    below = lax.rem(region + regions - 1, regions)

    def at(yy, xx):
        return (lax.rem(yy, NY) * NX + lax.rem(xx, NX), region)

    own_obs = pltpu.make_async_copy(obs, wide.at[1, 0, y, x], local_sem.at[0])
    own_inn = pltpu.make_async_copy(inn, wide.at[1, 1, y, x], local_sem.at[1])
    own_cols = pltpu.make_async_copy(
        states.at[:, pl.ds(pl.multiple_of(member * CELLS, CELLS), CELLS)], cols.at[member], local_sem.at[2]
    )
    own_obs.start()
    own_inn.start()
    own_cols.start()

    barrier = pltpu.get_barrier_semaphore()
    for k in range(1, GROUP):
        pl.semaphore_signal(barrier, inc=1, device_id=at(y + k // NX, x + k % NX), device_id_type=MESH)
    for other in (above, below):
        pl.semaphore_signal(barrier, inc=1, device_id=(member, other), device_id_type=MESH)
    pl.semaphore_wait(barrier, GROUP + 1)

    def cut(q):
        return pl.ds(q * QUART, QUART)

    def remote(source, target, send, recv, device):
        return pltpu.make_async_remote_copy(
            src_ref=source, dst_ref=target, send_sem=send, recv_sem=recv, device_id=device, device_id_type=MESH
        )

    def line(slot, q, d):
        if q % 2 == 0:
            return wide.at[slot, :, y, lax.rem(x + d, NX), :, cut(q)]
        return wide.at[slot, :, lax.rem(y + d, NY), x, :, cut(q)]

    def plane(slot, q, d, kind=slice(None)):
        if q % 2 == 0:
            return wide.at[slot, kind, lax.rem(y + d, NY), :, :, cut(q)]
        return wide.at[slot, kind, :, lax.rem(x + d, NX), :, cut(q)]

    def along(q, hop, d):
        return at(y, x + d) if (q + hop) % 2 == 0 else at(y + d, x)

    def first(q, d):
        piece = line(1, q, 0)
        return remote(piece, piece, g_send.at[q, d - 1], g_recv.at[q, d - 1], along(q, 0, d))

    def second(q, d, kind):
        piece, n = plane(1, q, 0, kind), 2 + d + kind
        return remote(piece, piece, g_send.at[q, n], g_recv.at[q, n], along(q, 1, d))

    def relay(q, d):
        piece, n = plane(1, q, 4 - d, d // 2), 7 + d // 2
        return remote(piece, piece, g_send.at[q, n], g_recv.at[q, n], along(q, 1, d))

    def piece_of(slot, piece):
        if piece == 0:
            return wide.at[slot, :, y, x]
        if piece < 13:
            return line(slot, (piece - 1) // 3, (piece - 1) % 3 + 1)
        return plane(slot, (piece - 13) // 6, (piece - 13) % 6 // 2 + 1, (piece - 13) % 2)

    def pass_on(piece, slot, n):
        return remote(
            piece_of(1, piece), piece_of(slot, piece), f_send.at[n, piece], f_recv.at[n, piece],
            (member, above if n == 0 else below),
        )

    def cells_in(k, part):
        yy, xx = lax.rem(y + k // NX, NY), lax.rem(x + k % NX, NX)
        target = yy * NX + xx
        place = pl.multiple_of(target * CELLS + part * PART_IN, PART_IN)
        return remote(
            states.at[:, pl.ds(place, PART_IN)], cols.at[member, :, pl.ds(part * PART_IN, PART_IN)],
            a_send.at[part, k - 1], a_recv.at[part, k - 1], (target, region),
        )

    def cells_out(part, k):
        yy, xx = lax.rem(y + k // NX, NY), lax.rem(x + k % NX, NX)
        target = yy * NX + xx
        begin, size = (n * BLK for n in PARTS[part])
        place = pl.multiple_of(member * CELLS + begin, BLK)
        return remote(
            result.at[target, :, pl.ds(begin, size)], out.at[:, pl.ds(place, size)],
            o_send.at[part, k - 1], o_recv.at[part, k - 1], (target, region),
        )

    def both(piece):
        pass_on(piece, 0, 0).start()
        pass_on(piece, 2, 1).start()

    def lines(pair):
        for d in (1, 3, 2):
            for q in pair:
                first(q, d).wait_recv()
                both(3 * q + 4 - d)
        for late in (0, 1):
            for d in (1, 3):
                for q in pair:
                    second(q, d, (d // 2 + late) % 2).start()

    def planes_near(pair, onward):
        for late in (0, 1):
            for d in (1, 3):
                for q in pair:
                    kind = (d // 2 + late) % 2
                    second(q, d, kind).wait_recv()
                    if not late:
                        relay(q, d).start()
                    if q in onward:
                        both(13 + 6 * q + 2 * (3 - d) + kind)

    def planes_far(pair, held=()):
        for q in pair:
            for d in (1, 3):
                relay(q, d).wait_recv()
                both(13 + 6 * q + 2 + d // 2)
            if q in held:
                for piece in (0, 1, 4, 5):
                    both(13 + 6 * q + piece)

    def states_to(begin, end):
        for n in range(begin, end):
            cells_in(ORDER[n % (GROUP - 1)], n // (GROUP - 1)).start()

    own_obs.wait()
    own_inn.wait()
    for pair in ((0, 1), (2, 3)):
        for d in (1, 3, 2):
            for q in pair:
                first(q, d).start()
    both(0)
    lines((0, 1))
    lines((2, 3))
    states_to(0, EARLY[0])

    start = member * CB
    ids = lists[...] - (region - 1) * OB
    used = lax.broadcasted_iota(jnp.int32, (L, BLK), 0) < counts[...]
    weights = jnp.where(used, taper[...], 0.0) * (1.0 / (MEMBERS - 1.0))
    lane_of = lax.broadcasted_iota(jnp.int32, (CB, BLK), 1)
    mine = (lane_of == start + lax.broadcasted_iota(jnp.int32, (CB, BLK), 0)).astype(jnp.float32)
    for b in range(3 * OB):
        total = jnp.sum(jnp.where(ids == b, weights, 0.0), axis=0, keepdims=True)
        table[b] = jnp.broadcast_to(jnp.sum(mine * total, axis=1, keepdims=True), (CB, BLK))

    def products(runs):
        base = 0
        for slot, begin, many in runs:
            def block(b, carry, slot=slot, begin=begin, base=base):
                at_b = pl.ds(pl.multiple_of((begin + b) * BLK, BLK), BLK)
                o = wide[slot, 0, :, :, :, at_b].reshape(MEMBERS, BLK)
                o_hi, o_lo = split(o - jnp.mean(o, axis=0, keepdims=True))
                i_hi, i_lo = split(wide[slot, 1, :, :, :, at_b].reshape(MEMBERS, BLK))
                g[base + b] = lax.dot_general(
                    jnp.concatenate([i_hi, i_lo, i_hi], axis=1), jnp.concatenate([o_hi, o_hi, o_lo], axis=1),
                    (((1,), (1,)), ((), ())), preferred_element_type=jnp.float32,
                )
                return carry

            lax.fori_loop(0, many, block, 0, unroll=True)
            base += many

    def add(runs, new=False, blocks=range(CB)):
        rows = [slot * OB + begin + b for slot, begin, many in runs for b in range(many)]

        def strip(i, carry):
            at_i = pl.ds(pl.multiple_of(i * 8, 8), 8)
            lanes = [pl.ds(k * BLK, BLK) for k in range(MEMBERS // BLK)]
            parts = [[g[b, at_i, lane] for lane in lanes] for b in range(len(rows))]
            for c in blocks:
                sums = [None if new else w[c, at_i, lane] for lane in lanes]
                for row, part in zip(rows, parts):
                    weight = jnp.broadcast_to(table[row, pl.ds(c, 1), :], (8, BLK))
                    sums = [p * weight if old is None else old + p * weight for old, p in zip(sums, part)]
                for lane, total in zip(lanes, sums):
                    w[c, at_i, lane] = total
            return carry

        lax.fori_loop(0, MEMBERS // 8, strip, 0, unroll=2)

    def window(*runs):
        products(runs)
        add(runs)

    near, far = 2 - 2 * core, 2 * core

    def arrived(slot, pieces):
        for piece in pieces:
            target = piece_of(slot, piece)
            remote(
                target, target, f_send.at[slot // 2, piece], f_recv.at[slot // 2, piece], (member, above)
            ).wait_recv()

    early = (*range(7), *range(13, 25))
    planes_near((0, 1), (0, 1))
    states_to(EARLY[0], EARLY[1])
    planes_far((0, 1))
    products([(1, 0, 4)])
    planes_near((2, 3), (2,))
    states_to(EARLY[1], EARLY[2])
    add([(1, 0, 4)], True)
    planes_far((2, 3), (3,))
    states_to(EARLY[2], INS * (GROUP - 1))
    arrived(near, early)
    window((near, 0, 4))
    arrived(near, (*range(7, 13), *range(25, 37)))
    window((1, 4, 4), (near, 4, 4))
    arrived(far, early)
    window((far, 0, 4))

    def centre(c, carry):
        at_c = pl.ds(pl.multiple_of(c * BLK, BLK), BLK)
        a = cols[:, :, at_c].reshape(MEMBERS, BLK)
        hi, lo = split(a - jnp.mean(a, axis=0, keepdims=True))
        cells_hl[c] = jnp.concatenate([hi, lo], axis=1)
        return carry

    def cells_here(part):
        for k in range(1, GROUP):
            cells_in(k, part).wait_recv()
        lax.fori_loop(part * (CB // INS), (part + 1) * (CB // INS), centre, 0)

    own_cols.wait()
    for part in range(INS_EARLY):
        cells_here(part)
    arrived(far, (*range(7, 10), *range(25, 31)))
    window((far, 4, 2))
    arrived(far, (*range(10, 13), *range(31, 37)))
    products([(far, 6, 2)])

    for part, (begin, many) in enumerate(PARTS):
        def finish(c, carry):
            at_c = pl.ds(pl.multiple_of(c * BLK, BLK), BLK)
            hi, lo = split(w[c])
            a = cells_hl[c]
            both_ = jnp.dot(hi, a, preferred_element_type=jnp.float32)
            low = jnp.dot(lo, a[:, :BLK], preferred_element_type=jnp.float32)
            inc = both_[:, :BLK] + (both_[:, BLK:] + low)
            result[:, :, at_c] = cols[:, :, at_c] + inc.reshape(GROUP, ROWS, BLK)
            return carry

        if begin * INS % CB == 0 and begin * INS // CB >= INS_EARLY:
            cells_here(begin * INS // CB)
        add([(far, 6, 2)], blocks=range(begin, begin + many))
        lax.fori_loop(begin, begin + many, finish, 0)
        for k in ORDER:
            cells_out(part, k).start()
    place = pl.multiple_of(member * CELLS, CELLS)
    keep = pltpu.make_async_copy(result.at[member], out.at[:, pl.ds(place, CELLS)], local_sem.at[3])
    keep.start()

    for q in range(4):
        for d in (1, 2, 3):
            first(q, d).wait_send()
        for d in (1, 3):
            second(q, d, 0).wait_send()
            second(q, d, 1).wait_send()
            relay(q, d).wait_send()
    for piece in range(37):
        pass_on(piece, 0, 0).wait_send()
        pass_on(piece, 2, 1).wait_send()
    for part in range(INS):
        for k in range(1, GROUP):
            cells_in(k, part).wait_send()
    for part in range(SENDS):
        for k in range(1, GROUP):
            cells_out(part, k).wait()
    keep.wait()


def local(states, obs_ens, innovation, lists, counts, taper):
    hbm = pl.BlockSpec(memory_space=pl.ANY)
    vmem = pl.BlockSpec(memory_space=pltpu.VMEM)
    dma = pltpu.SemaphoreType.DMA
    return pl.pallas_call(
        kernel,
        out_shape=pltpu.VMEM(states.shape, jnp.float32),
        in_specs=[hbm, hbm, hbm, vmem, vmem, vmem],
        out_specs=vmem,
        scratch_shapes=[
            pltpu.VMEM((3, 2, NY, NX, ROWS, OBS), jnp.float32),
            pltpu.VMEM((GROUP, ROWS, CELLS), jnp.float32),
            pltpu.VMEM((CB, MEMBERS, 2 * BLK), jnp.bfloat16),
            pltpu.VMEM((OB, MEMBERS, MEMBERS), jnp.float32),
            pltpu.VMEM((CB, MEMBERS, MEMBERS), jnp.float32),
            pltpu.VMEM((3 * OB, CB, BLK), jnp.float32),
            pltpu.VMEM((GROUP, ROWS, CELLS), jnp.float32),
            dma((4,)),
            dma((4, 9)),
            dma((4, 9)),
            dma((2, 37)),
            dma((2, 37)),
            dma((INS, GROUP - 1)),
            dma((INS, GROUP - 1)),
            dma((SENDS, GROUP - 1)),
            dma((SENDS, GROUP - 1)),
        ],
        compiler_params=pltpu.CompilerParams(
            collective_id=0, has_side_effects=True, vmem_limit_bytes=58 * 2**20
        ),
        name="analysis",
    )(states, obs_ens, innovation, lists.T, counts.reshape(1, -1), taper.T)


def solution(mesh):
    return jax.shard_map(
        local,
        mesh=mesh,
        in_specs=(
            P("member", "region"),
            P("member", "region"),
            P("member", "region"),
            P("region", None),
            P("region"),
            P("region", None),
        ),
        out_specs=P("member", "region"),
        check_vma=False,
    )
```

```python
import jax
import jax.numpy as jnp
from jax import lax
from jax.experimental import pallas as pl
from jax.experimental.pallas import tpu as pltpu
from jax.sharding import PartitionSpec as P

MESH = pl.DeviceIdType.MESH
BLK = 128
NX = 4
NY = 4
GROUP = NX * NY
ROWS = 32
MEMBERS = 512
CELLS = 1024
CB = CELLS // BLK
OBS = 1024
OB = OBS // BLK
QUART = OBS // 4
INS = 2
PART_IN = CELLS // INS
L = 24
PARTS = ((0, 1), (1, 1), (2, 2), (4, 2), (6, 2))
SENDS = len(PARTS)
EARLY = (0, 0, 0)
INS_EARLY = 1
ORDER = (1, 4, 3, 12, 5, 15, 7, 13, 2, 8, 6, 9, 14, 11, 10)


def split(value):
    high = value.astype(jnp.bfloat16)
    return high, (value - high.astype(jnp.float32)).astype(jnp.bfloat16)


def kernel(
    states, obs, inn, lists, counts, taper, out,
    wide, cols, cells_hl, g, w, table, result,
    local_sem, g_send, g_recv, f_send, f_recv, a_send, a_recv, o_send, o_recv,
):
    member = lax.axis_index("member")
    region = lax.axis_index("region")
    regions = lax.axis_size("region")
    y, x = member // NX, member % NX
    core = region % 2
    above = lax.rem(region + 1, regions)
    below = lax.rem(region + regions - 1, regions)

    def at(yy, xx):
        return (lax.rem(yy, NY) * NX + lax.rem(xx, NX), region)

    own_obs = pltpu.make_async_copy(obs, wide.at[1, 0, y, x], local_sem.at[0])
    own_inn = pltpu.make_async_copy(inn, wide.at[1, 1, y, x], local_sem.at[1])
    own_cols = pltpu.make_async_copy(
        states.at[:, pl.ds(pl.multiple_of(member * CELLS, CELLS), CELLS)], cols.at[member], local_sem.at[2]
    )
    own_obs.start()
    own_inn.start()
    own_cols.start()

    barrier = pltpu.get_barrier_semaphore()
    for k in range(1, GROUP):
        pl.semaphore_signal(barrier, inc=1, device_id=at(y + k // NX, x + k % NX), device_id_type=MESH)
    for other in (above, below):
        pl.semaphore_signal(barrier, inc=1, device_id=(member, other), device_id_type=MESH)
    pl.semaphore_wait(barrier, GROUP + 1)

    def cut(q):
        return pl.ds(q * QUART, QUART)

    def remote(source, target, send, recv, device):
        return pltpu.make_async_remote_copy(
            src_ref=source, dst_ref=target, send_sem=send, recv_sem=recv, device_id=device, device_id_type=MESH
        )

    def line(slot, q, d):
        if q % 2 == 0:
            return wide.at[slot, :, y, lax.rem(x + d, NX), :, cut(q)]
        return wide.at[slot, :, lax.rem(y + d, NY), x, :, cut(q)]

    def plane(slot, q, d, kind=slice(None)):
        if q % 2 == 0:
            return wide.at[slot, kind, lax.rem(y + d, NY), :, :, cut(q)]
        return wide.at[slot, kind, :, lax.rem(x + d, NX), :, cut(q)]

    def along(q, hop, d):
        return at(y, x + d) if (q + hop) % 2 == 0 else at(y + d, x)

    def first(q, d):
        piece = line(1, q, 0)
        return remote(piece, piece, g_send.at[q, d - 1], g_recv.at[q, d - 1], along(q, 0, d))

    def second(q, d, kind):
        piece, n = plane(1, q, 0, kind), 2 + d + kind
        return remote(piece, piece, g_send.at[q, n], g_recv.at[q, n], along(q, 1, d))

    def relay(q, d):
        piece, n = plane(1, q, 4 - d, d // 2), 7 + d // 2
        return remote(piece, piece, g_send.at[q, n], g_recv.at[q, n], along(q, 1, d))

    def piece_of(slot, piece):
        if piece == 0:
            return wide.at[slot, :, y, x]
        if piece < 13:
            return line(slot, (piece - 1) // 3, (piece - 1) % 3 + 1)
        return plane(slot, (piece - 13) // 6, (piece - 13) % 6 // 2 + 1, (piece - 13) % 2)

    def pass_on(piece, slot, n):
        return remote(
            piece_of(1, piece), piece_of(slot, piece), f_send.at[n, piece], f_recv.at[n, piece],
            (member, above if n == 0 else below),
        )

    def cells_in(k, part):
        yy, xx = lax.rem(y + k // NX, NY), lax.rem(x + k % NX, NX)
        target = yy * NX + xx
        place = pl.multiple_of(target * CELLS + part * PART_IN, PART_IN)
        return remote(
            states.at[:, pl.ds(place, PART_IN)], cols.at[member, :, pl.ds(part * PART_IN, PART_IN)],
            a_send.at[part, k - 1], a_recv.at[part, k - 1], (target, region),
        )

    def cells_out(part, k):
        yy, xx = lax.rem(y + k // NX, NY), lax.rem(x + k % NX, NX)
        target = yy * NX + xx
        begin, size = (n * BLK for n in PARTS[part])
        place = pl.multiple_of(member * CELLS + begin, BLK)
        return remote(
            result.at[target, :, pl.ds(begin, size)], out.at[:, pl.ds(place, size)],
            o_send.at[part, k - 1], o_recv.at[part, k - 1], (target, region),
        )

    far_region = lax.rem(region + regions - 1 + 2 * core, regions)
    near_region = region + 1 - 2 * core

    def both(piece):
        for n, slot, device in ((1 - core, 2 - 2 * core, far_region), (core, 2 * core, near_region)):
            remote(
                piece_of(1, piece), piece_of(slot, piece), f_send.at[n, piece], f_recv.at[n, piece], (member, device)
            ).start()

    def lines(pair):
        for d in (1, 3, 2):
            for q in pair:
                first(q, d).wait_recv()
                both(3 * q + 4 - d)
        for late in (0, 1):
            for d in (1, 3):
                for q in pair:
                    second(q, d, (d // 2 + late) % 2).start()

    def planes_near(pair, onward):
        for late in (0, 1):
            for d in (1, 3):
                for q in pair:
                    kind = (d // 2 + late) % 2
                    second(q, d, kind).wait_recv()
                    if not late:
                        relay(q, d).start()
                    if q in onward:
                        both(13 + 6 * q + 2 * (3 - d) + kind)

    def planes_far(pair, held=()):
        for q in pair:
            for d in (1, 3):
                relay(q, d).wait_recv()
                both(13 + 6 * q + 2 + d // 2)
            if q in held:
                for piece in (0, 1, 4, 5):
                    both(13 + 6 * q + piece)

    def states_to(begin, end):
        for n in range(begin, end):
            cells_in(ORDER[n % (GROUP - 1)], n // (GROUP - 1)).start()

    own_obs.wait()
    own_inn.wait()
    for pair in ((0, 1), (2, 3)):
        for d in (1, 3, 2):
            for q in pair:
                first(q, d).start()
    both(0)
    lines((0, 1))
    lines((2, 3))
    states_to(0, EARLY[0])

    start = member * CB
    ids = lists[...] - (region - 1) * OB
    used = lax.broadcasted_iota(jnp.int32, (L, BLK), 0) < counts[...]
    weights = jnp.where(used, taper[...], 0.0) * (1.0 / (MEMBERS - 1.0))
    lane_of = lax.broadcasted_iota(jnp.int32, (CB, BLK), 1)
    mine = (lane_of == start + lax.broadcasted_iota(jnp.int32, (CB, BLK), 0)).astype(jnp.float32)
    for b in range(3 * OB):
        total = jnp.sum(jnp.where(ids == b, weights, 0.0), axis=0, keepdims=True)
        table[b] = jnp.broadcast_to(jnp.sum(mine * total, axis=1, keepdims=True), (CB, BLK))

    def products(runs):
        base = 0
        for slot, begin, many in runs:
            def block(b, carry, slot=slot, begin=begin, base=base):
                at_b = pl.ds(pl.multiple_of((begin + b) * BLK, BLK), BLK)
                o = wide[slot, 0, :, :, :, at_b].reshape(MEMBERS, BLK)
                o_hi, o_lo = split(o - jnp.mean(o, axis=0, keepdims=True))
                i_hi, i_lo = split(wide[slot, 1, :, :, :, at_b].reshape(MEMBERS, BLK))
                g[base + b] = lax.dot_general(
                    jnp.concatenate([i_hi, i_lo, i_hi], axis=1), jnp.concatenate([o_hi, o_hi, o_lo], axis=1),
                    (((1,), (1,)), ((), ())), preferred_element_type=jnp.float32,
                )
                return carry

            lax.fori_loop(0, many, block, 0, unroll=True)
            base += many

    def add(runs, new=False, blocks=range(CB)):
        rows = [slot * OB + begin + b for slot, begin, many in runs for b in range(many)]

        def strip(i, carry):
            at_i = pl.ds(pl.multiple_of(i * 8, 8), 8)
            lanes = [pl.ds(k * BLK, BLK) for k in range(MEMBERS // BLK)]
            parts = [[g[b, at_i, lane] for lane in lanes] for b in range(len(rows))]
            for c in blocks:
                sums = [None if new else w[c, at_i, lane] for lane in lanes]
                for row, part in zip(rows, parts):
                    weight = jnp.broadcast_to(table[row, pl.ds(c, 1), :], (8, BLK))
                    sums = [p * weight if old is None else old + p * weight for old, p in zip(sums, part)]
                for lane, total in zip(lanes, sums):
                    w[c, at_i, lane] = total
            return carry

        lax.fori_loop(0, MEMBERS // 8, strip, 0, unroll=2)

    def window(*runs):
        products(runs)
        add(runs)

    near, far = 2 - 2 * core, 2 * core

    def arrived(slot, pieces):
        for piece in pieces:
            target = piece_of(slot, piece)
            remote(
                target, target, f_send.at[slot // 2, piece], f_recv.at[slot // 2, piece], (member, above)
            ).wait_recv()

    early = (*range(7), *range(13, 25))
    planes_near((0, 1), (0, 1))
    states_to(EARLY[0], EARLY[1])
    planes_far((0, 1))
    products([(1, 0, 4)])
    planes_near((2, 3), (2,))
    states_to(EARLY[1], EARLY[2])
    add([(1, 0, 4)], True)
    planes_far((2, 3), (3,))
    states_to(EARLY[2], INS * (GROUP - 1))
    arrived(near, early)
    window((near, 0, 4))
    arrived(near, (*range(7, 13), *range(25, 37)))
    window((1, 4, 4), (near, 4, 4))
    arrived(far, early)
    window((far, 0, 4))

    def centre(c, carry):
        at_c = pl.ds(pl.multiple_of(c * BLK, BLK), BLK)
        a = cols[:, :, at_c].reshape(MEMBERS, BLK)
        hi, lo = split(a - jnp.mean(a, axis=0, keepdims=True))
        cells_hl[c] = jnp.concatenate([hi, lo], axis=1)
        return carry

    def cells_here(part):
        for k in range(1, GROUP):
            cells_in(k, part).wait_recv()
        lax.fori_loop(part * (CB // INS), (part + 1) * (CB // INS), centre, 0)

    own_cols.wait()
    for part in range(INS_EARLY):
        cells_here(part)
    arrived(far, (*range(7, 10), *range(25, 31)))
    window((far, 4, 2))
    arrived(far, (*range(10, 13), *range(31, 37)))
    products([(far, 6, 2)])

    for part, (begin, many) in enumerate(PARTS):
        def finish(c, carry):
            at_c = pl.ds(pl.multiple_of(c * BLK, BLK), BLK)
            hi, lo = split(w[c])
            a = cells_hl[c]
            both_ = jnp.dot(hi, a, preferred_element_type=jnp.float32)
            low = jnp.dot(lo, a[:, :BLK], preferred_element_type=jnp.float32)
            inc = both_[:, :BLK] + (both_[:, BLK:] + low)
            result[:, :, at_c] = cols[:, :, at_c] + inc.reshape(GROUP, ROWS, BLK)
            return carry

        if begin * INS % CB == 0 and begin * INS // CB >= INS_EARLY:
            cells_here(begin * INS // CB)
        add([(far, 6, 2)], blocks=range(begin, begin + many))
        lax.fori_loop(begin, begin + many, finish, 0)
        for k in ORDER:
            cells_out(part, k).start()
    place = pl.multiple_of(member * CELLS, CELLS)
    keep = pltpu.make_async_copy(result.at[member], out.at[:, pl.ds(place, CELLS)], local_sem.at[3])
    keep.start()

    for q in range(4):
        for d in (1, 2, 3):
            first(q, d).wait_send()
        for d in (1, 3):
            second(q, d, 0).wait_send()
            second(q, d, 1).wait_send()
            relay(q, d).wait_send()
    for piece in range(37):
        pass_on(piece, 0, 0).wait_send()
        pass_on(piece, 2, 1).wait_send()
    for part in range(INS):
        for k in range(1, GROUP):
            cells_in(k, part).wait_send()
    for part in range(SENDS):
        for k in range(1, GROUP):
            cells_out(part, k).wait()
    keep.wait()


def local(states, obs_ens, innovation, lists, counts, taper):
    hbm = pl.BlockSpec(memory_space=pl.ANY)
    vmem = pl.BlockSpec(memory_space=pltpu.VMEM)
    dma = pltpu.SemaphoreType.DMA
    return pl.pallas_call(
        kernel,
        out_shape=pltpu.VMEM(states.shape, jnp.float32),
        in_specs=[hbm, hbm, hbm, vmem, vmem, vmem],
        out_specs=vmem,
        scratch_shapes=[
            pltpu.VMEM((3, 2, NY, NX, ROWS, OBS), jnp.float32),
            pltpu.VMEM((GROUP, ROWS, CELLS), jnp.float32),
            pltpu.VMEM((CB, MEMBERS, 2 * BLK), jnp.bfloat16),
            pltpu.VMEM((OB, MEMBERS, MEMBERS), jnp.float32),
            pltpu.VMEM((CB, MEMBERS, MEMBERS), jnp.float32),
            pltpu.VMEM((3 * OB, CB, BLK), jnp.float32),
            pltpu.VMEM((GROUP, ROWS, CELLS), jnp.float32),
            dma((4,)),
            dma((4, 9)),
            dma((4, 9)),
            dma((2, 37)),
            dma((2, 37)),
            dma((INS, GROUP - 1)),
            dma((INS, GROUP - 1)),
            dma((SENDS, GROUP - 1)),
            dma((SENDS, GROUP - 1)),
        ],
        compiler_params=pltpu.CompilerParams(
            collective_id=0, has_side_effects=True, vmem_limit_bytes=58 * 2**20
        ),
        name="analysis",
    )(states, obs_ens, innovation, lists.T, counts.reshape(1, -1), taper.T)


def solution(mesh):
    return jax.shard_map(
        local,
        mesh=mesh,
        in_specs=(
            P("member", "region"),
            P("member", "region"),
            P("member", "region"),
            P("region", None),
            P("region"),
            P("region", None),
        ),
        out_specs=P("member", "region"),
        check_vma=False,
    )
```

```python
import jax
import jax.numpy as jnp
from jax import lax
from jax.experimental import pallas as pl
from jax.experimental.pallas import tpu as pltpu
from jax.sharding import PartitionSpec as P

MESH = pl.DeviceIdType.MESH
BLK = 128
NX = 4
NY = 4
GROUP = NX * NY
ROWS = 32
MEMBERS = 512
CELLS = 1024
CB = CELLS // BLK
OBS = 1024
OB = OBS // BLK
QUART = OBS // 4
INS = 2
PART_IN = CELLS // INS
L = 24
PARTS = ((0, 1), (1, 1), (2, 2), (4, 2), (6, 2))
SENDS = len(PARTS)
EARLY = (0, 0, 8)
INS_EARLY = 1
CROSSED = tuple(13 + 6 * q + 2 * (3 - d) + d // 2 for q in (2, 3) for d in (1, 3))
ORDER = (1, 4, 3, 12, 5, 15, 7, 13, 2, 8, 6, 9, 14, 11, 10)


def split(value):
    high = value.astype(jnp.bfloat16)
    return high, (value - high.astype(jnp.float32)).astype(jnp.bfloat16)


def kernel(
    states, obs, inn, lists, counts, taper, out,
    wide, cols, cells_hl, g, w, table, result,
    local_sem, g_send, g_recv, f_send, f_recv, x_send, x_recv, a_send, a_recv, o_send, o_recv,
):
    member = lax.axis_index("member")
    region = lax.axis_index("region")
    regions = lax.axis_size("region")
    y, x = member // NX, member % NX
    core = region % 2
    above = lax.rem(region + 1, regions)
    below = lax.rem(region + regions - 1, regions)

    def at(yy, xx):
        return (lax.rem(yy, NY) * NX + lax.rem(xx, NX), region)

    own_obs = pltpu.make_async_copy(obs, wide.at[1, 0, y, x], local_sem.at[0])
    own_inn = pltpu.make_async_copy(inn, wide.at[1, 1, y, x], local_sem.at[1])
    own_cols = pltpu.make_async_copy(
        states.at[:, pl.ds(pl.multiple_of(member * CELLS, CELLS), CELLS)], cols.at[member], local_sem.at[2]
    )
    own_obs.start()
    own_inn.start()
    own_cols.start()

    barrier = pltpu.get_barrier_semaphore()
    for k in range(1, GROUP):
        pl.semaphore_signal(barrier, inc=1, device_id=at(y + k // NX, x + k % NX), device_id_type=MESH)
    for other in (above, below):
        pl.semaphore_signal(barrier, inc=1, device_id=(member, other), device_id_type=MESH)
    pl.semaphore_wait(barrier, GROUP + 1)

    def cut(q):
        return pl.ds(q * QUART, QUART)

    def remote(source, target, send, recv, device):
        return pltpu.make_async_remote_copy(
            src_ref=source, dst_ref=target, send_sem=send, recv_sem=recv, device_id=device, device_id_type=MESH
        )

    def line(slot, q, d):
        if q % 2 == 0:
            return wide.at[slot, :, y, lax.rem(x + d, NX), :, cut(q)]
        return wide.at[slot, :, lax.rem(y + d, NY), x, :, cut(q)]

    def plane(slot, q, d, kind=slice(None)):
        if q % 2 == 0:
            return wide.at[slot, kind, lax.rem(y + d, NY), :, :, cut(q)]
        return wide.at[slot, kind, :, lax.rem(x + d, NX), :, cut(q)]

    def along(q, hop, d):
        return at(y, x + d) if (q + hop) % 2 == 0 else at(y + d, x)

    def first(q, d):
        piece = line(1, q, 0)
        return remote(piece, piece, g_send.at[q, d - 1], g_recv.at[q, d - 1], along(q, 0, d))

    def second(q, d, kind):
        piece, n = plane(1, q, 0, kind), 2 + d + kind
        return remote(piece, piece, g_send.at[q, n], g_recv.at[q, n], along(q, 1, d))

    def relay(q, d):
        piece, n = plane(1, q, 4 - d, d // 2), 7 + d // 2
        return remote(piece, piece, g_send.at[q, n], g_recv.at[q, n], along(q, 1, d))

    def piece_of(slot, piece):
        if piece == 0:
            return wide.at[slot, :, y, x]
        if piece < 13:
            return line(slot, (piece - 1) // 3, (piece - 1) % 3 + 1)
        return plane(slot, (piece - 13) // 6, (piece - 13) % 6 // 2 + 1, (piece - 13) % 2)

    far_region = lax.rem(region + regions - 1 + 2 * core, regions)
    near_region = region + 1 - 2 * core

    def to_far(piece):
        n, slot = 1 - core, 2 - 2 * core
        return remote(
            piece_of(1, piece), piece_of(slot, piece), f_send.at[n, piece], f_recv.at[n, piece], (member, far_region)
        )

    def to_near(piece):
        n, slot = core, 2 * core
        return remote(
            piece_of(1, piece), piece_of(slot, piece), f_send.at[n, piece], f_recv.at[n, piece], (member, near_region)
        )

    def across(q, d):
        piece, n = plane(2 * core, q, 0, d // 2), (q - 2) * 2 + d // 2
        return remote(piece, piece, x_send.at[n], x_recv.at[n], along(q, 1, d))

    def cells_in(k, part):
        yy, xx = lax.rem(y + k // NX, NY), lax.rem(x + k % NX, NX)
        target = yy * NX + xx
        place = pl.multiple_of(target * CELLS + part * PART_IN, PART_IN)
        return remote(
            states.at[:, pl.ds(place, PART_IN)], cols.at[member, :, pl.ds(part * PART_IN, PART_IN)],
            a_send.at[part, k - 1], a_recv.at[part, k - 1], (target, region),
        )

    def cells_out(part, k):
        yy, xx = lax.rem(y + k // NX, NY), lax.rem(x + k % NX, NX)
        target = yy * NX + xx
        begin, size = (n * BLK for n in PARTS[part])
        place = pl.multiple_of(member * CELLS + begin, BLK)
        return remote(
            result.at[target, :, pl.ds(begin, size)], out.at[:, pl.ds(place, size)],
            o_send.at[part, k - 1], o_recv.at[part, k - 1], (target, region),
        )

    def both(piece):
        if piece not in CROSSED:
            to_far(piece).start()
        to_near(piece).start()

    def lines(pair):
        for d in (1, 3, 2):
            for q in pair:
                first(q, d).wait_recv()
                both(3 * q + 4 - d)
        for late in (0, 1):
            for d in (1, 3):
                for q in pair:
                    second(q, d, (d // 2 + late) % 2).start()

    def planes_near(pair, onward):
        for late in (0, 1):
            for d in (1, 3):
                for q in pair:
                    kind = (d // 2 + late) % 2
                    second(q, d, kind).wait_recv()
                    if not late:
                        relay(q, d).start()
                    if q in onward:
                        both(13 + 6 * q + 2 * (3 - d) + kind)

    def planes_far(pair, held=()):
        for q in pair:
            for d in (1, 3):
                relay(q, d).wait_recv()
                both(13 + 6 * q + 2 + d // 2)
            if q in held:
                for piece in (0, 1, 4, 5):
                    both(13 + 6 * q + piece)

    def states_to(begin, end):
        for n in range(begin, end):
            cells_in(ORDER[n % (GROUP - 1)], n // (GROUP - 1)).start()

    own_obs.wait()
    own_inn.wait()
    for pair in ((0, 1), (2, 3)):
        for d in (1, 3, 2):
            for q in pair:
                first(q, d).start()
    both(0)
    lines((0, 1))
    lines((2, 3))
    states_to(0, EARLY[0])

    start = member * CB
    ids = lists[...] - (region - 1) * OB
    used = lax.broadcasted_iota(jnp.int32, (L, BLK), 0) < counts[...]
    weights = jnp.where(used, taper[...], 0.0) * (1.0 / (MEMBERS - 1.0))
    lane_of = lax.broadcasted_iota(jnp.int32, (CB, BLK), 1)
    mine = (lane_of == start + lax.broadcasted_iota(jnp.int32, (CB, BLK), 0)).astype(jnp.float32)
    for b in range(3 * OB):
        total = jnp.sum(jnp.where(ids == b, weights, 0.0), axis=0, keepdims=True)
        table[b] = jnp.broadcast_to(jnp.sum(mine * total, axis=1, keepdims=True), (CB, BLK))

    def products(runs):
        base = 0
        for slot, begin, many in runs:
            def block(b, carry, slot=slot, begin=begin, base=base):
                at_b = pl.ds(pl.multiple_of((begin + b) * BLK, BLK), BLK)
                o = wide[slot, 0, :, :, :, at_b].reshape(MEMBERS, BLK)
                o_hi, o_lo = split(o - jnp.mean(o, axis=0, keepdims=True))
                i_hi, i_lo = split(wide[slot, 1, :, :, :, at_b].reshape(MEMBERS, BLK))
                g[base + b] = lax.dot_general(
                    jnp.concatenate([i_hi, i_lo, i_hi], axis=1), jnp.concatenate([o_hi, o_hi, o_lo], axis=1),
                    (((1,), (1,)), ((), ())), preferred_element_type=jnp.float32,
                )
                return carry

            lax.fori_loop(0, many, block, 0, unroll=True)
            base += many

    def add(runs, new=False, blocks=range(CB)):
        rows = [slot * OB + begin + b for slot, begin, many in runs for b in range(many)]

        def strip(i, carry):
            at_i = pl.ds(pl.multiple_of(i * 8, 8), 8)
            lanes = [pl.ds(k * BLK, BLK) for k in range(MEMBERS // BLK)]
            parts = [[g[b, at_i, lane] for lane in lanes] for b in range(len(rows))]
            for c in blocks:
                sums = [None if new else w[c, at_i, lane] for lane in lanes]
                for row, part in zip(rows, parts):
                    weight = jnp.broadcast_to(table[row, pl.ds(c, 1), :], (8, BLK))
                    sums = [p * weight if old is None else old + p * weight for old, p in zip(sums, part)]
                for lane, total in zip(lanes, sums):
                    w[c, at_i, lane] = total
            return carry

        lax.fori_loop(0, MEMBERS // 8, strip, 0, unroll=4)

    def window(*runs):
        products(runs)
        add(runs)

    near, far = 2 - 2 * core, 2 * core

    def arrived(slot, pieces):
        for piece in pieces:
            target = piece_of(slot, piece)
            remote(
                target, target, f_send.at[slot // 2, piece], f_recv.at[slot // 2, piece], (member, above)
            ).wait_recv()

    early = (*range(7), *range(13, 25))
    planes_near((0, 1), (0, 1))
    states_to(EARLY[0], EARLY[1])
    planes_far((0, 1))
    products([(1, 0, 4)])
    planes_near((2, 3), (2,))
    states_to(EARLY[1], EARLY[2])
    add([(1, 0, 4)], True)
    planes_far((2, 3), (3,))
    arrived(far, (0, *range(7, 13)))
    for q in (2, 3):
        for d in (1, 3):
            across(q, d).start()
    states_to(EARLY[2], INS * (GROUP - 1))
    arrived(near, early)
    window((near, 0, 4))
    arrived(near, (*range(7, 13), *range(25, 37)))
    window((1, 4, 4), (near, 4, 4))
    arrived(far, early[1:])
    window((far, 0, 4))

    def centre(c, carry):
        at_c = pl.ds(pl.multiple_of(c * BLK, BLK), BLK)
        a = cols[:, :, at_c].reshape(MEMBERS, BLK)
        hi, lo = split(a - jnp.mean(a, axis=0, keepdims=True))
        cells_hl[c] = jnp.concatenate([hi, lo], axis=1)
        return carry

    def cells_here(part):
        for k in range(1, GROUP):
            cells_in(k, part).wait_recv()
        lax.fori_loop(part * (CB // INS), (part + 1) * (CB // INS), centre, 0)

    own_cols.wait()
    for part in range(INS_EARLY):
        cells_here(part)
    arrived(far, [piece for piece in range(25, 31) if piece not in CROSSED])
    for d in (1, 3):
        across(2, d).wait_recv()
    window((far, 4, 2))
    arrived(far, [piece for piece in range(31, 37) if piece not in CROSSED])
    for d in (1, 3):
        across(3, d).wait_recv()
    products([(far, 6, 2)])

    for part, (begin, many) in enumerate(PARTS):
        def finish(c, carry):
            at_c = pl.ds(pl.multiple_of(c * BLK, BLK), BLK)
            hi, lo = split(w[c])
            a = cells_hl[c]
            both_ = jnp.dot(hi, a, preferred_element_type=jnp.float32)
            low = jnp.dot(lo, a[:, :BLK], preferred_element_type=jnp.float32)
            inc = both_[:, :BLK] + (both_[:, BLK:] + low)
            result[:, :, at_c] = cols[:, :, at_c] + inc.reshape(GROUP, ROWS, BLK)
            return carry

        if begin * INS % CB == 0 and begin * INS // CB >= INS_EARLY:
            cells_here(begin * INS // CB)
        add([(far, 6, 2)], blocks=range(begin, begin + many))
        lax.fori_loop(begin, begin + many, finish, 0)
        for k in ORDER:
            cells_out(part, k).start()
    place = pl.multiple_of(member * CELLS, CELLS)
    keep = pltpu.make_async_copy(result.at[member], out.at[:, pl.ds(place, CELLS)], local_sem.at[3])
    keep.start()

    for q in range(4):
        for d in (1, 2, 3):
            first(q, d).wait_send()
        for d in (1, 3):
            second(q, d, 0).wait_send()
            second(q, d, 1).wait_send()
            relay(q, d).wait_send()
    for piece in range(37):
        if piece not in CROSSED:
            to_far(piece).wait_send()
        to_near(piece).wait_send()
    for q in (2, 3):
        for d in (1, 3):
            across(q, d).wait_send()
    for part in range(INS):
        for k in range(1, GROUP):
            cells_in(k, part).wait_send()
    for part in range(SENDS):
        for k in range(1, GROUP):
            cells_out(part, k).wait()
    keep.wait()


def local(states, obs_ens, innovation, lists, counts, taper):
    hbm = pl.BlockSpec(memory_space=pl.ANY)
    vmem = pl.BlockSpec(memory_space=pltpu.VMEM)
    dma = pltpu.SemaphoreType.DMA
    return pl.pallas_call(
        kernel,
        out_shape=pltpu.VMEM(states.shape, jnp.float32),
        in_specs=[hbm, hbm, hbm, vmem, vmem, vmem],
        out_specs=vmem,
        scratch_shapes=[
            pltpu.VMEM((3, 2, NY, NX, ROWS, OBS), jnp.float32),
            pltpu.VMEM((GROUP, ROWS, CELLS), jnp.float32),
            pltpu.VMEM((CB, MEMBERS, 2 * BLK), jnp.bfloat16),
            pltpu.VMEM((OB, MEMBERS, MEMBERS), jnp.float32),
            pltpu.VMEM((CB, MEMBERS, MEMBERS), jnp.float32),
            pltpu.VMEM((3 * OB, CB, BLK), jnp.float32),
            pltpu.VMEM((GROUP, ROWS, CELLS), jnp.float32),
            dma((4,)),
            dma((4, 9)),
            dma((4, 9)),
            dma((2, 37)),
            dma((2, 37)),
            dma((4,)),
            dma((4,)),
            dma((INS, GROUP - 1)),
            dma((INS, GROUP - 1)),
            dma((SENDS, GROUP - 1)),
            dma((SENDS, GROUP - 1)),
        ],
        compiler_params=pltpu.CompilerParams(
            collective_id=0, has_side_effects=True, vmem_limit_bytes=58 * 2**20
        ),
        name="analysis",
    )(states, obs_ens, innovation, lists.T, counts.reshape(1, -1), taper.T)


def solution(mesh):
    return jax.shard_map(
        local,
        mesh=mesh,
        in_specs=(
            P("member", "region"),
            P("member", "region"),
            P("member", "region"),
            P("region", None),
            P("region"),
            P("region", None),
        ),
        out_specs=P("member", "region"),
        check_vma=False,
    )
```
